32 devices in a mesh: ctx: 8 (over z, core), head: 4 (over y, x).
Axes of the slice: x: 2, y: 2, z: 4, core: 2. Of those that a mesh axis runs over, the one named last changes fastest.
Arguments:
- queries: bfloat16 [2048, 32, 128], P('ctx', 'head'), may hold values from -8 to 8
- key_proj: bfloat16 [2048, 4, 128], P(('ctx', 'head')), may hold values from -8 to 8
- value_proj: bfloat16 [2048, 4, 128], P(('ctx', 'head')), may hold values from -6 to 6
- out_grad: bfloat16 [2048, 32, 128], P('ctx', 'head'), may hold values from -6 to 6
- tile_order: int32 [16], replicated, may hold values from 0 to 15, each once
- doc_tiles: int32 [4], replicated, may hold values from 1 to 8, 16 in all
Outputs:
- attended: bfloat16 [2048, 32, 128], P('ctx', 'head')
- query_grad: bfloat16 [2048, 32, 128], P('ctx', 'head')
- key_grad: bfloat16 [2048, 4, 128], P(('ctx', 'head'))
- value_grad: bfloat16 [2048, 4, 128], P(('ctx', 'head'))
The draws below stay inside these ranges and needn't reach their ends.
Inputs may be any that keep to these rules, and one draw needn't show every extreme that they name: `tile_order`: a permutation of the 16 tiles. `doc_tiles`: positive lengths in tiles summing to 16.
All inputs are finite; a program needn't handle non-finite values.
Results may differ from the reference program's by a relative error of at most 0.02.
Values may be sent and summed in bfloat16 or wider, within the bound.
A program may use at most 64 MiB of HBM per device.

```python
import math
import jax
import jax.numpy as jnp
import numpy as np
from jax import lax

HD = 128
GROUP = 8
TILE = 128
DOCS = 4
SEQ = 2048
TILES = 16
KV_HEADS = 4
Q_HEADS = 32


def draw_queries(key, part):
    noise_key = jax.random.fold_in(key, 31)
    values = jnp.clip(jax.random.normal(noise_key, (SEQ, Q_HEADS, HD), jnp.float32), -6.0, 6.0)
    return values.astype(jnp.bfloat16)


def draw_key_proj(key, part):
    noise_key = jax.random.fold_in(key, 53)
    values = jnp.clip(jax.random.normal(noise_key, (SEQ, KV_HEADS, HD), jnp.float32), -6.0, 6.0)
    return values.astype(jnp.bfloat16)


def levels(key, extent, pieces, least, high):
    gain, own = 1.0, jax.random.fold_in(key, 6)
    for axis_at, blocks in pieces:
        heights = jnp.exp(jax.random.uniform(jax.random.fold_in(own, axis_at), (blocks,), jnp.float32, least / len(pieces), high / len(pieces)))
        gain = gain * jnp.repeat(heights, extent[axis_at] // blocks).reshape([-1 if axis == axis_at else 1 for axis in range(len(extent))])
    return gain


def split_up(number_of, total, most, skew):
    loads = [(1 << 20) // math.isqrt(rank ** skew) + 1 for rank in range(2, number_of + 1)]
    surplus, given = total - most - (number_of - 1), [1] * (number_of - 1)
    while surplus > 0:
        candidates = [i for i in range(number_of - 1) if given[i] < most]
        mass, budget = sum([loads[i] for i in candidates]), surplus
        for i in candidates:
            extra = min(most - given[i], max(1, budget * loads[i] // mass), surplus)
            given[i] = given[i] + extra
            surplus = surplus - extra
    return np.array([most] + given)


def ragged(stream_key, amount, total, limit, lean):
    if amount == 2:
        one = jax.random.randint(stream_key, (), max(1, total - limit), min(limit, total - 1) + 1)
        return jnp.stack([one, total - one])
    sizes = jnp.asarray(split_up(amount, total, limit, lean), jnp.int32)
    twos = (amount - 1) // 2
    source_of, sink = sizes[1:1 + 2 * twos:2], sizes[2:2 + 2 * twos:2]
    room = jnp.minimum(source_of - 1, limit - sink)
    shifted = jax.random.randint(jax.random.fold_in(stream_key, 1), (twos,), 0, 1 << 20) % (room + 1)
    sizes = sizes.at[1:1 + 2 * twos:2].set(source_of - shifted).at[2:2 + 2 * twos:2].set(sink + shifted)
    return sizes[jax.random.permutation(jax.random.fold_in(stream_key, 2), amount)]


def gaussian(key, shape, width, limit, cuts=(), kind=jnp.bfloat16):
    result = width * jax.random.normal(key, shape, jnp.float32)
    if cuts:
        result = result * levels(key, shape, cuts, -0.22, 0.18)
    return jnp.clip(result, -limit, limit).astype(kind)


def setup_inputs(seed: int = 0) -> dict:
    streams_of = jax.random.split(jax.random.key(seed), 7)
    queries = draw_queries(jax.random.fold_in(streams_of[6], 71), 0)
    key_proj = draw_key_proj(jax.random.fold_in(streams_of[6], 71), 0)
    value_proj = gaussian(streams_of[2], (SEQ, KV_HEADS, HD), 1.0, 6.0, ((0, 32),))
    out_grad = gaussian(streams_of[3], (SEQ, Q_HEADS, HD), 1.0, 6.0, ((0, 8), (1, 4)))
    tile_order = jax.random.permutation(streams_of[4], TILES).astype(jnp.int32)
    doc_tiles = ragged(streams_of[5], DOCS, TILES, TILES // 2, 0).astype(jnp.int32)
    return {"queries": queries, "key_proj": key_proj, "value_proj": value_proj, "out_grad": out_grad, "tile_order": tile_order, "doc_tiles": doc_tiles}


NEG = -1e+30

def layout(tile_order, doc_tiles):
    doc_ends = jnp.cumsum(doc_tiles).astype(jnp.int32)
    tile_doc = lax.optimization_barrier(jnp.sum((tile_order[:, None] >= doc_ends[None, :]).astype(jnp.int32), axis=1))
    offsets = jnp.arange(TILE, dtype=jnp.int32)
    positions = (tile_order[:, None] * TILE + offsets[None, :]).reshape(-1)
    documents = jnp.repeat(tile_doc, TILE)
    return (positions, documents)

def reference(queries, key_proj, value_proj, out_grad, tile_order, doc_tiles):
    positions, documents = layout(tile_order, doc_tiles)
    allowed = (documents[:, None] == documents[None, :]) & (positions[None, :] <= positions[:, None])
    score_scale = 1.0 / math.sqrt(HD)
    grouped_q = queries.reshape(SEQ, KV_HEADS, GROUP, HD).transpose(1, 2, 0, 3)
    grouped_g = out_grad.reshape(SEQ, KV_HEADS, GROUP, HD).transpose(1, 2, 0, 3)
    key_heads = key_proj.transpose(1, 0, 2)
    value_heads = value_proj.transpose(1, 0, 2)

    def one_head(query_rows, grad_rows, key_rows, value_rows):
        scores = jnp.dot(query_rows, key_rows.T, preferred_element_type=jnp.float32) * score_scale
        row_top = lax.optimization_barrier(jnp.max(jnp.where(allowed, scores, NEG), axis=1))
        weights = jnp.where(allowed, jnp.exp(scores - row_top[:, None]), 0.0)
        row_sum = lax.optimization_barrier(jnp.sum(weights, axis=1))
        attended = (jnp.dot(weights.astype(jnp.bfloat16), value_rows, preferred_element_type=jnp.float32) / row_sum[:, None]).astype(jnp.bfloat16)
        log_sum = row_top + jnp.log(row_sum)
        probs = jnp.where(allowed, jnp.exp(scores - log_sum[:, None]), 0.0)
        value_term = jnp.dot(probs.astype(jnp.bfloat16).T, grad_rows, preferred_element_type=jnp.float32)
        dprobs = jnp.dot(grad_rows, value_rows.T, preferred_element_type=jnp.float32)
        delta = lax.optimization_barrier(jnp.sum(grad_rows.astype(jnp.float32) * attended.astype(jnp.float32), axis=1))
        dscores = (probs * (dprobs - delta[:, None])).astype(jnp.bfloat16)
        query_grad = (jnp.dot(dscores, key_rows, preferred_element_type=jnp.float32) * score_scale).astype(jnp.bfloat16)
        key_term = jnp.dot(dscores.T, query_rows, preferred_element_type=jnp.float32)
        return (attended, query_grad, key_term, value_term)

    def per_group(inputs):
        query_group, grad_group, key_rows, value_rows = inputs

        def inner(carried, pair):
            attended, query_grad, key_term, value_term = one_head(pair[0], pair[1], key_rows, value_rows)
            return ((carried[0] + key_term, carried[1] + value_term), (attended, query_grad))
        start = (jnp.zeros((SEQ, HD), jnp.float32), jnp.zeros((SEQ, HD), jnp.float32))
        sums, outputs = lax.scan(inner, start, (query_group, grad_group))
        return (outputs[0], outputs[1], (sums[0] * score_scale).astype(jnp.bfloat16), sums[1].astype(jnp.bfloat16))
    attended, query_grad, key_grad, value_grad = lax.map(per_group, (grouped_q, grouped_g, key_heads, value_heads))
    attended = attended.transpose(2, 0, 1, 3).reshape(SEQ, Q_HEADS, HD)
    query_grad = query_grad.transpose(2, 0, 1, 3).reshape(SEQ, Q_HEADS, HD)
    key_grad = key_grad.transpose(1, 0, 2)
    value_grad = value_grad.transpose(1, 0, 2)
    return (attended, query_grad, key_grad, value_grad)
```

```python
import functools
import math

import jax
import jax.numpy as jnp
from jax import lax
from jax.experimental import pallas as pl
from jax.experimental.pallas import tpu as pltpu
from jax.sharding import PartitionSpec as P

TILE = 128
NEG = -1e30
MESH = pl.DeviceIdType.MESH
VMEM_LIMIT = 48 * 1024 * 1024


def peers(n_ctx, n_head):
    ctx = lax.axis_index("ctx")
    head = lax.axis_index("head")
    core = lax.rem(ctx, 2)
    rail = lax.div(ctx, 2)
    n_rail = n_ctx // 2
    sibling = rail * 2 + (1 - core)
    return ctx, head, core, rail, n_rail, sibling


def entry_barrier(ctx, head, core, rail, n_rail, sibling, n_head):
    barrier = pltpu.get_barrier_semaphore()
    for d in range(1, n_head):
        pl.semaphore_signal(
            barrier, inc=1, device_id=(ctx, lax.rem(head + d, n_head)), device_id_type=MESH
        )
    for d in range(1, n_rail):
        pl.semaphore_signal(
            barrier,
            inc=1,
            device_id=(lax.rem(rail + d, n_rail) * 2 + core, head),
            device_id_type=MESH,
        )
    pl.semaphore_signal(barrier, inc=1, device_id=(sibling, head), device_id_type=MESH)
    pl.semaphore_wait(barrier, n_head - 1 + n_rail - 1 + 1)


def remote(src, dst, send, recv, ctx, head):
    return pltpu.make_async_remote_copy(
        src_ref=src,
        dst_ref=dst,
        send_sem=send,
        recv_sem=recv,
        device_id=(ctx, head),
        device_id_type=MESH,
    )


def gather_kernel(n_ctx, n_head, k_ref, v_ref, out_ref, turned, head_sems, rail_sems, sib_sems, fwd_sems):
    ctx, head, core, rail, n_rail, sibling = peers(n_ctx, n_head)
    for g in range(n_head):
        turned[g, 0] = k_ref[:, g * 128 : (g + 1) * 128]
        turned[g, 1] = v_ref[:, g * 128 : (g + 1) * 128]
    out_ref[:, ctx, head] = turned[head]
    entry_barrier(ctx, head, core, rail, n_rail, sibling, n_head)

    def head_copy(d):
        target = lax.rem(head + d, n_head)
        return remote(
            turned.at[target], out_ref.at[:, ctx, head], head_sems.at[0, d], head_sems.at[1, d], ctx, target
        )

    for d in range(1, n_head):
        head_copy(d).start()

    def rail_copy(dz, d):
        source = lax.rem(head + n_head - d, n_head)
        target = lax.rem(rail + dz, n_rail) * 2 + core
        block = out_ref.at[:, ctx, source]
        return remote(block, block, rail_sems.at[0, dz, d], rail_sems.at[1, dz, d], target, head)

    def sib_copy(d):
        source = lax.rem(head + n_head - d, n_head)
        block = out_ref.at[:, ctx, source]
        return remote(block, block, sib_sems.at[0, d], sib_sems.at[1, d], sibling, head)

    def fwd_copy(dz):
        block = out_ref.at[:, lax.rem(rail + n_rail - dz, n_rail) * 2 + core]
        return remote(block, block, fwd_sems.at[0, dz], fwd_sems.at[1, dz], sibling, head)

    for d in range(n_head):
        if d > 0:
            head_copy(d).wait_recv()
        for dz in range(1, n_rail):
            rail_copy(dz, d).start()
        sib_copy(d).start()
    for dz in range(1, n_rail):
        for d in range(n_head):
            rail_copy(dz, d).wait_recv()
        fwd_copy(dz).start()
    for d in range(1, n_head):
        head_copy(d).wait_send()
    for d in range(n_head):
        for dz in range(1, n_rail):
            rail_copy(dz, d).wait_send()
        sib_copy(d).wait()
    for dz in range(1, n_rail):
        fwd_copy(dz).wait()


def reduce_kernel(
    n_ctx, n_head, part_ref, k_ref, v_ref, sib_in, summed, rail_in, turned, head_in,
    sib_sems, rail_sems, head_sems,
):
    ctx, head, core, rail, n_rail, sibling = peers(n_ctx, n_head)
    entry_barrier(ctx, head, core, rail, n_rail, sibling, n_head)

    def rail_of(dz):
        return lax.rem(rail + dz, n_rail)

    def sib_copy(dz):
        return remote(
            part_ref.at[:, rail_of(dz) * 2 + (1 - core)],
            sib_in.at[dz],
            sib_sems.at[0, dz],
            sib_sems.at[1, dz],
            sibling,
            head,
        )

    def rail_copy(dz):
        return remote(
            summed.at[dz], rail_in.at[dz], rail_sems.at[0, dz], rail_sems.at[1, dz],
            rail_of(dz) * 2 + core, head,
        )

    def head_copy(d):
        target = lax.rem(head + d, n_head)
        return remote(
            turned.at[target], head_in.at[d], head_sems.at[0, d], head_sems.at[1, d], ctx, target
        )

    order = list(range(n_rail - 1, 0, -1)) + [0]
    for dz in order:
        sib_copy(dz).start()
    total = None
    for dz in order:
        sib_copy(dz).wait_recv()
        own = part_ref[:, rail_of(dz) * 2 + core].astype(jnp.float32)
        both = own + sib_in[dz].astype(jnp.float32)
        if dz > 0:
            summed[dz] = both.astype(jnp.bfloat16)
            rail_copy(dz).start()
        else:
            total = both
    for dz in range(1, n_rail):
        rail_copy(dz).wait_recv()
        total = total + rail_in[dz].astype(jnp.float32)
    scale = 1.0 / math.sqrt(128)
    for g in range(n_head):
        turned[g, 0] = (total[0, g] * scale).astype(jnp.bfloat16)
        turned[g, 1] = total[1, g].astype(jnp.bfloat16)
    for d in range(1, n_head):
        head_copy(d).start()
    head_in[0] = turned[head]
    for d in range(1, n_head):
        head_copy(d).wait_recv()
    for g in range(n_head):
        place = lax.rem(head - g + n_head, n_head)
        k_ref[:, g * 128 : (g + 1) * 128] = head_in[place, 0]
        v_ref[:, g * 128 : (g + 1) * 128] = head_in[place, 1]
    for dz in range(n_rail):
        sib_copy(dz).wait_send()
    for dz in range(1, n_rail):
        rail_copy(dz).wait_send()
    for d in range(1, n_head):
        head_copy(d).wait_send()


def dot(a, b):
    return jnp.dot(a, b, preferred_element_type=jnp.float32)


def attention_kernel(
    tiles, group, docs, order_ref, docs_ref, q_ref, g_ref, kv_ref, o_ref, dq_ref, dkv_ref,
    slot_of, k_t, v_t, q_t, g_t, g_s, g_st, scores, weights, o_t, dq_t, dkv, apart,
):
    step = pl.program_id(0)
    per_shard = pl.num_programs(0)
    rows = TILE * group
    scale = 1.0 / math.sqrt(128)

    @pl.when(step == 0)
    def _():
        for s in range(tiles):
            slot_of[order_ref[s]] = s

        @pl.loop(0, tiles)
        def _(s):
            k_t[s] = kv_ref[0, s].T
            v_t[s] = kv_ref[1, s].T

        dkv[...] = jnp.zeros_like(dkv)
        key = lax.broadcasted_iota(jnp.int32, (TILE, rows), 0)
        row = lax.broadcasted_iota(jnp.int32, (TILE, rows), 1)
        apart[...] = key - lax.div(row, group)

    mine = order_ref[lax.axis_index("ctx") * per_shard + step]
    end, first = 0, 0
    for d in range(docs):
        end = end + docs_ref[d]
        first = jnp.where(end <= mine, end, first)
    count = mine - first + 1
    turns = lax.div(count + 1, 2)

    q_t[...] = q_ref[...].T
    g_t[...] = g_ref[...].T

    def pair(j):
        near = slot_of[mine - 2 * j]
        far = slot_of[jnp.maximum(mine - 2 * j - 1, 0)]
        return near, far

    def cut(j):
        near_cut = jnp.where(j == 0, 0, TILE)
        far_cut = jnp.where(2 * j + 1 < count, TILE, -TILE)
        return near_cut, far_cut

    def top_turn(j, top):
        for half, (slot, limit) in enumerate(zip(pair(j), cut(j))):
            s = dot(kv_ref[0, slot], q_t[...])
            s = jnp.where(apart[...] <= limit, s, NEG)
            scores[j, half * TILE : (half + 1) * TILE] = s
            top = jnp.maximum(top, jnp.max(s.reshape(TILE // 8, 8, rows), axis=0))
        return top

    top = lax.fori_loop(0, turns, top_turn, jnp.full((8, rows), NEG, jnp.float32))
    top = jnp.max(top, axis=0, keepdims=True)

    o_t[...] = jnp.zeros_like(o_t)

    def sum_turn(j, total):
        slots = pair(j)
        w = jnp.exp((scores[j] - top) * scale)
        total = total + jnp.sum(w.reshape(2 * TILE // 8, 8, rows), axis=0)
        w = w.astype(jnp.bfloat16)
        weights[j] = w
        values = jnp.concatenate([v_t[slots[0]], v_t[slots[1]]], axis=1)
        o_t[...] += dot(values, w)
        return total

    total = lax.fori_loop(0, turns, sum_turn, jnp.zeros((8, rows), jnp.float32))
    inverse = 1.0 / jnp.sum(total, axis=0, keepdims=True)
    out_t = (o_t[...] * inverse).astype(jnp.bfloat16)
    o_ref[...] = out_t.T
    grads = g_t[...].astype(jnp.float32)
    delta = jnp.sum(grads * out_t.astype(jnp.float32), axis=0, keepdims=True) * inverse
    scaled = (grads * inverse).astype(jnp.bfloat16)
    g_st[...] = scaled
    g_s[...] = scaled.T
    dq_t[...] = jnp.zeros_like(dq_t)

    def grad_turn(j, _):
        slots = pair(j)
        parts = []
        for half, slot in enumerate(slots):
            w = weights[j, half * TILE : (half + 1) * TILE]
            dp = dot(kv_ref[1, slot], g_st[...])
            ds = (w.astype(jnp.float32) * (dp - delta)).astype(jnp.bfloat16)
            parts.append(ds)
            dkv[0, slot] += dot(ds, q_ref[...])
            dkv[1, slot] += dot(w, g_s[...])
        keys = jnp.concatenate([k_t[slots[0]], k_t[slots[1]]], axis=1)
        dq_t[...] += dot(keys, jnp.concatenate(parts, axis=0))
        return 0

    lax.fori_loop(0, turns, grad_turn, 0)
    dq_ref[...] = (dq_t[...] * scale).astype(jnp.bfloat16).T

    @pl.when(step == per_shard - 1)
    def _():
        dkv_ref[...] = dkv[...].astype(jnp.bfloat16)


def body(n_ctx, n_head, queries, key_proj, value_proj, out_grad, tile_order, doc_tiles):
    row_count, group, depth = queries.shape
    share, kv_heads, _ = key_proj.shape
    tiles = tile_order.shape[0]
    docs = doc_tiles.shape[0]
    n_rail = n_ctx // 2
    bf16, f32 = jnp.bfloat16, jnp.float32
    vmem = pl.BlockSpec(memory_space=pltpu.VMEM)
    dma = pltpu.SemaphoreType.DMA

    rows_kv = pl.pallas_call(
        functools.partial(gather_kernel, n_ctx, n_head),
        out_shape=jax.ShapeDtypeStruct((2, n_ctx, n_head, share, depth), bf16),
        in_specs=[vmem, vmem],
        out_specs=vmem,
        scratch_shapes=[
            pltpu.VMEM((n_head, 2, share, depth), bf16),
            dma((2, n_head)),
            dma((2, n_rail, n_head)),
            dma((2, n_head)),
            dma((2, n_rail)),
        ],
        compiler_params=pltpu.CompilerParams(
            collective_id=0, has_side_effects=True, vmem_limit_bytes=VMEM_LIMIT
        ),
        name="gather_rows",
    )(key_proj.reshape(share, kv_heads * depth), value_proj.reshape(share, kv_heads * depth))

    rows = TILE * group
    per_shard = row_count // TILE
    most = tiles // 4
    smem = pl.BlockSpec(memory_space=pltpu.SMEM)
    tile_spec = pl.BlockSpec((rows, depth), lambda t: (t, 0))
    attended, query_grad, partial = pl.pallas_call(
        functools.partial(attention_kernel, tiles, group, docs),
        grid=(per_shard,),
        out_shape=(
            jax.ShapeDtypeStruct((row_count * group, depth), bf16),
            jax.ShapeDtypeStruct((row_count * group, depth), bf16),
            jax.ShapeDtypeStruct((2, tiles, TILE, depth), bf16),
        ),
        in_specs=[smem, smem, tile_spec, tile_spec, vmem],
        out_specs=(tile_spec, tile_spec, vmem),
        scratch_shapes=[
            pltpu.SMEM((tiles,), jnp.int32),
            pltpu.VMEM((tiles, depth, TILE), bf16),
            pltpu.VMEM((tiles, depth, TILE), bf16),
            pltpu.VMEM((depth, rows), bf16),
            pltpu.VMEM((depth, rows), bf16),
            pltpu.VMEM((rows, depth), bf16),
            pltpu.VMEM((depth, rows), bf16),
            pltpu.VMEM((most, 2 * TILE, rows), f32),
            pltpu.VMEM((most, 2 * TILE, rows), bf16),
            pltpu.VMEM((depth, rows), f32),
            pltpu.VMEM((depth, rows), f32),
            pltpu.VMEM((2, tiles, TILE, depth), f32),
            pltpu.VMEM((TILE, rows), jnp.int32),
        ],
        compiler_params=pltpu.CompilerParams(vmem_limit_bytes=VMEM_LIMIT),
        name="attention_tiles",
    )(
        tile_order,
        doc_tiles,
        queries.reshape(row_count * group, depth),
        out_grad.reshape(row_count * group, depth),
        rows_kv.reshape(2, tiles, TILE, depth),
    )

    key_grad, value_grad = pl.pallas_call(
        functools.partial(reduce_kernel, n_ctx, n_head),
        out_shape=(
            jax.ShapeDtypeStruct((share, kv_heads * depth), bf16),
            jax.ShapeDtypeStruct((share, kv_heads * depth), bf16),
        ),
        in_specs=[vmem],
        out_specs=(vmem, vmem),
        scratch_shapes=[
            pltpu.VMEM((n_rail, 2, n_head, share, depth), bf16),
            pltpu.VMEM((n_rail, 2, n_head, share, depth), bf16),
            pltpu.VMEM((n_rail, 2, n_head, share, depth), bf16),
            pltpu.VMEM((n_head, 2, share, depth), bf16),
            pltpu.VMEM((n_head, 2, share, depth), bf16),
            dma((2, n_rail)),
            dma((2, n_rail)),
            dma((2, n_head)),
        ],
        compiler_params=pltpu.CompilerParams(
            collective_id=1, has_side_effects=True, vmem_limit_bytes=VMEM_LIMIT
        ),
        name="sum_gradients",
    )(partial.reshape(2, n_ctx, n_head, share, depth))

    return (
        attended.reshape(row_count, group, depth),
        query_grad.reshape(row_count, group, depth),
        key_grad.reshape(share, kv_heads, depth),
        value_grad.reshape(share, kv_heads, depth),
    )


def solution(mesh):
    in_specs = (
        P("ctx", "head", None),
        P(("ctx", "head"), None, None),
        P(("ctx", "head"), None, None),
        P("ctx", "head", None),
        P(),
        P(),
    )
    out_specs = (
        P("ctx", "head", None),
        P("ctx", "head", None),
        P(("ctx", "head"), None, None),
        P(("ctx", "head"), None, None),
    )
    return jax.shard_map(
        functools.partial(body, mesh.shape["ctx"], mesh.shape["head"]),
        mesh=mesh,
        in_specs=in_specs,
        out_specs=out_specs,
        check_vma=False,
    )
```

```python
import functools
import math

import jax
import jax.numpy as jnp
from jax import lax
from jax.experimental import pallas as pl
from jax.experimental.pallas import tpu as pltpu
from jax.sharding import PartitionSpec as P

TILE = 128
NEG = -1e30
MESH = pl.DeviceIdType.MESH
VMEM_LIMIT = 48 * 1024 * 1024


def peers(n_ctx, n_head):
    ctx = lax.axis_index("ctx")
    head = lax.axis_index("head")
    core = lax.rem(ctx, 2)
    rail = lax.div(ctx, 2)
    n_rail = n_ctx // 2
    sibling = rail * 2 + (1 - core)
    return ctx, head, core, rail, n_rail, sibling


def entry_barrier(ctx, head, core, rail, n_rail, sibling, n_head):
    barrier = pltpu.get_barrier_semaphore()
    for d in range(1, n_head):
        pl.semaphore_signal(
            barrier, inc=1, device_id=(ctx, lax.rem(head + d, n_head)), device_id_type=MESH
        )
    for d in range(1, n_rail):
        pl.semaphore_signal(
            barrier,
            inc=1,
            device_id=(lax.rem(rail + d, n_rail) * 2 + core, head),
            device_id_type=MESH,
        )
    pl.semaphore_signal(barrier, inc=1, device_id=(sibling, head), device_id_type=MESH)
    pl.semaphore_wait(barrier, n_head - 1 + n_rail - 1 + 1)


def remote(src, dst, send, recv, ctx, head):
    return pltpu.make_async_remote_copy(
        src_ref=src,
        dst_ref=dst,
        send_sem=send,
        recv_sem=recv,
        device_id=(ctx, head),
        device_id_type=MESH,
    )


def gather_kernel(
    n_ctx, n_head, k_ref, v_ref, out_ref, turned, head_sems, right_sems, left_sems, sib_sems
):
    ctx, head, core, rail, n_rail, sibling = peers(n_ctx, n_head)
    for g in range(n_head):
        turned[g, 0] = k_ref[:, g * 128 : (g + 1) * 128]
        turned[g, 1] = v_ref[:, g * 128 : (g + 1) * 128]
    out_ref[:, ctx, head] = turned[head]
    entry_barrier(ctx, head, core, rail, n_rail, sibling, n_head)

    def head_copy(d):
        target = lax.rem(head + d, n_head)
        return remote(
            turned.at[target], out_ref.at[:, ctx, head], head_sems.at[0, d], head_sems.at[1, d], ctx, target
        )

    for d in range(1, n_head):
        head_copy(d).start()

    def block_of(source, d):
        return out_ref.at[:, source * 2 + core, lax.rem(head + n_head - d, n_head)]

    def line_copy(way, hops, d):
        sems = right_sems if way > 0 else left_sems
        block = block_of(jnp.clip(rail - way * hops, 0, n_rail - 1), d)
        target = jnp.clip(rail + way, 0, n_rail - 1) * 2 + core
        return remote(block, block, sems.at[0, hops, d], sems.at[1, hops, d], target, head)

    def line_recv(way, hops, d):
        sems = right_sems if way > 0 else left_sems
        block = block_of(jnp.clip(rail - way * hops, 0, n_rail - 1), d)
        source = jnp.clip(rail - way, 0, n_rail - 1) * 2 + core
        return remote(block, block, sems.at[0, hops - 1, d], sems.at[1, hops - 1, d], source, head)

    def sib_copy(source, d):
        block = block_of(source, d)
        return remote(block, block, sib_sems.at[0, source, d], sib_sems.at[1, source, d], sibling, head)

    def room(way):
        return n_rail - 1 - rail if way > 0 else rail

    for d in range(n_head):
        if d > 0:
            head_copy(d).wait_recv()
        for way in (1, -1):
            @pl.when(room(way) > 0)
            def _():
                line_copy(way, 0, d).start()
        sib_copy(rail, d).start()
    for hops in range(1, n_rail):
        for d in range(n_head):
            for way in (1, -1):
                @pl.when(room(-way) >= hops)
                def _():
                    line_recv(way, hops, d).wait_recv()

                    @pl.when(room(way) > 0)
                    def _():
                        line_copy(way, hops, d).start()
                    sib_copy(rail - way * hops, d).start()
    for d in range(1, n_head):
        head_copy(d).wait_send()
    for d in range(n_head):
        for hops in range(n_rail - 1):
            for way in (1, -1):
                @pl.when((room(way) > 0) & (room(-way) >= hops))
                def _():
                    line_copy(way, hops, d).wait_send()
        for source in range(n_rail):
            sib_copy(source, d).wait_send()
            block = out_ref.at[:, source * 2 + 1 - core, lax.rem(head + n_head - d, n_head)]
            remote(
                block, block, sib_sems.at[0, source, d], sib_sems.at[1, source, d], sibling, head
            ).wait_recv()


def reduce_kernel(
    n_ctx, n_head, part_ref, k_ref, v_ref, sib_in, right_out, left_out, right_in, left_in,
    turned, head_in, sib_sems, right_sems, left_sems, head_sems,
):
    ctx, head, core, rail, n_rail, sibling = peers(n_ctx, n_head)
    scale = 1.0 / math.sqrt(128)
    entry_barrier(ctx, head, core, rail, n_rail, sibling, n_head)

    def sib_copy(dest):
        return remote(
            part_ref.at[:, dest * 2 + (1 - core)],
            sib_in.at[dest],
            sib_sems.at[0, dest],
            sib_sems.at[1, dest],
            sibling,
            head,
        )

    def line_copy(way, dest, g):
        sems, out, into = (
            (right_sems, right_out, right_in) if way > 0 else (left_sems, left_out, left_in)
        )
        target = jnp.clip(rail + way, 0, n_rail - 1) * 2 + core
        return remote(
            out.at[dest, g], into.at[dest, g], sems.at[0, dest, g], sems.at[1, dest, g], target, head
        )

    def head_copy(g, place):
        return remote(
            turned.at[g], head_in.at[place], head_sems.at[0, g], head_sems.at[1, place], ctx, g
        )

    def pair_sum(dest, g):
        own = part_ref[:, dest * 2 + core, g].astype(jnp.float32)
        return own + sib_in[dest, :, g].astype(jnp.float32)

    order = []
    for i in range(n_rail):
        for dest in (n_rail - 1 - i, i):
            if dest not in order:
                order.append(dest)
    for dest in order:
        sib_copy(dest).start()

    def send_on(way, dest):
        out, into = (right_out, right_in) if way > 0 else (left_out, left_in)
        first = rail == (0 if way > 0 else n_rail - 1)

        @pl.loop(0, n_head)
        def _(g):
            @pl.when(first)
            def _():
                out[dest, g] = pair_sum(dest, g).astype(jnp.bfloat16)

            @pl.when(jnp.logical_not(first))
            def _():
                line_copy(way, dest, g).wait_recv()
                both = pair_sum(dest, g) + into[dest, g].astype(jnp.float32)
                out[dest, g] = both.astype(jnp.bfloat16)
            line_copy(way, dest, g).start()

    arrived = set()
    for i in range(n_rail):
        for way, dest in ((1, n_rail - 1 - i), (-1, i)):
            if dest not in arrived:
                arrived.add(dest)
                sib_copy(dest).wait_recv()
            if way > 0 and dest > 0:
                @pl.when(dest > rail)
                def _():
                    send_on(1, dest)
            if way < 0 and dest < n_rail - 1:
                @pl.when(dest < rail)
                def _():
                    send_on(-1, dest)

    @pl.loop(0, n_head)
    def _(g):
        @pl.when(rail > 0)
        def _():
            line_copy(1, rail, g).wait_recv()

        @pl.when(rail < n_rail - 1)
        def _():
            line_copy(-1, rail, g).wait_recv()
        def finish(total):
            turned[g, 0] = (total[0] * scale).astype(jnp.bfloat16)
            turned[g, 1] = total[1].astype(jnp.bfloat16)

        @pl.when(rail == 0)
        def _():
            finish(pair_sum(rail, g) + left_in[rail, g].astype(jnp.float32))

        @pl.when(rail == n_rail - 1)
        def _():
            finish(pair_sum(rail, g) + right_in[rail, g].astype(jnp.float32))

        @pl.when((rail > 0) & (rail < n_rail - 1))
        def _():
            sides = right_in[rail, g].astype(jnp.float32) + left_in[rail, g].astype(jnp.float32)
            finish(pair_sum(rail, g) + sides)

        @pl.when(g != head)
        def _():
            head_copy(g, head).start()

    head_in[head] = turned[head]
    for g in range(n_head):
        @pl.when(g != head)
        def _():
            head_copy(g, g).wait_recv()
        k_ref[:, g * 128 : (g + 1) * 128] = head_in[g, 0]
        v_ref[:, g * 128 : (g + 1) * 128] = head_in[g, 1]
    for g in range(n_head):
        @pl.when(g != head)
        def _():
            head_copy(g, head).wait_send()
    for dest in range(n_rail):
        sib_copy(dest).wait_send()

        @pl.loop(0, n_head)
        def _(g):
            @pl.when(dest > rail)
            def _():
                line_copy(1, dest, g).wait_send()

            @pl.when(dest < rail)
            def _():
                line_copy(-1, dest, g).wait_send()


def dot(a, b):
    return jnp.dot(a, b, preferred_element_type=jnp.float32)


def attention_kernel(
    tiles, group, docs, order_ref, docs_ref, q_ref, g_ref, kv_ref, o_ref, dq_ref, dkv_ref,
    slot_of, k_t, v_t, q_t, g_t, g_s, g_st, scores, weights, o_t, dq_t, dkv, apart,
):
    step = pl.program_id(0)
    per_shard = pl.num_programs(0)
    rows = TILE * group
    scale = 1.0 / math.sqrt(128)

    @pl.when(step == 0)
    def _():
        for s in range(tiles):
            slot_of[order_ref[s]] = s

        @pl.loop(0, tiles)
        def _(s):
            k_t[s] = kv_ref[0, s].T
            v_t[s] = kv_ref[1, s].T

        dkv[...] = jnp.zeros_like(dkv)
        key = lax.broadcasted_iota(jnp.int32, (TILE, rows), 0)
        row = lax.broadcasted_iota(jnp.int32, (TILE, rows), 1)
        apart[...] = key - lax.div(row, group)

    mine = order_ref[lax.axis_index("ctx") * per_shard + step]
    end, first = 0, 0
    for d in range(docs):
        end = end + docs_ref[d]
        first = jnp.where(end <= mine, end, first)
    count = mine - first + 1
    turns = lax.div(count + 1, 2)

    q_t[...] = q_ref[...].T
    g_t[...] = g_ref[...].T

    def pair(j):
        near = slot_of[mine - 2 * j]
        far = slot_of[jnp.maximum(mine - 2 * j - 1, 0)]
        return near, far

    def cut(j):
        near_cut = jnp.where(j == 0, 0, TILE)
        far_cut = jnp.where(2 * j + 1 < count, TILE, -TILE)
        return near_cut, far_cut

    def top_turn(j, top):
        for half, (slot, limit) in enumerate(zip(pair(j), cut(j))):
            s = dot(kv_ref[0, slot], q_t[...])
            s = jnp.where(apart[...] <= limit, s, NEG)
            scores[j, half * TILE : (half + 1) * TILE] = s
            top = jnp.maximum(top, jnp.max(s.reshape(TILE // 8, 8, rows), axis=0))
        return top

    top = lax.fori_loop(0, turns, top_turn, jnp.full((8, rows), NEG, jnp.float32))
    top = jnp.max(top, axis=0, keepdims=True)

    o_t[...] = jnp.zeros_like(o_t)

    def sum_turn(j, total):
        slots = pair(j)
        w = jnp.exp((scores[j] - top) * scale)
        total = total + jnp.sum(w.reshape(2 * TILE // 8, 8, rows), axis=0)
        w = w.astype(jnp.bfloat16)
        weights[j] = w
        values = jnp.concatenate([v_t[slots[0]], v_t[slots[1]]], axis=1)
        o_t[...] += dot(values, w)
        return total

    total = lax.fori_loop(0, turns, sum_turn, jnp.zeros((8, rows), jnp.float32))
    inverse = 1.0 / jnp.sum(total, axis=0, keepdims=True)
    out_t = (o_t[...] * inverse).astype(jnp.bfloat16)
    o_ref[...] = out_t.T
    grads = g_t[...].astype(jnp.float32)
    delta = jnp.sum(grads * out_t.astype(jnp.float32), axis=0, keepdims=True) * inverse
    scaled = (grads * inverse).astype(jnp.bfloat16)
    g_st[...] = scaled
    g_s[...] = scaled.T
    dq_t[...] = jnp.zeros_like(dq_t)

    def grad_turn(j, _):
        slots = pair(j)
        parts = []
        for half, slot in enumerate(slots):
            w = weights[j, half * TILE : (half + 1) * TILE]
            dp = dot(kv_ref[1, slot], g_st[...])
            ds = (w.astype(jnp.float32) * (dp - delta)).astype(jnp.bfloat16)
            parts.append(ds)
            dkv[0, slot] += dot(ds, q_ref[...])
            dkv[1, slot] += dot(w, g_s[...])
        keys = jnp.concatenate([k_t[slots[0]], k_t[slots[1]]], axis=1)
        dq_t[...] += dot(keys, jnp.concatenate(parts, axis=0))
        return 0

    lax.fori_loop(0, turns, grad_turn, 0)
    dq_ref[...] = (dq_t[...] * scale).astype(jnp.bfloat16).T

    @pl.when(step == per_shard - 1)
    def _():
        dkv_ref[...] = dkv[...].astype(jnp.bfloat16)


def body(n_ctx, n_head, queries, key_proj, value_proj, out_grad, tile_order, doc_tiles):
    row_count, group, depth = queries.shape
    share, kv_heads, _ = key_proj.shape
    tiles = tile_order.shape[0]
    docs = doc_tiles.shape[0]
    n_rail = n_ctx // 2
    bf16, f32 = jnp.bfloat16, jnp.float32
    vmem = pl.BlockSpec(memory_space=pltpu.VMEM)
    dma = pltpu.SemaphoreType.DMA

    rows_kv = pl.pallas_call(
        functools.partial(gather_kernel, n_ctx, n_head),
        out_shape=jax.ShapeDtypeStruct((2, n_ctx, n_head, share, depth), bf16),
        in_specs=[vmem, vmem],
        out_specs=vmem,
        scratch_shapes=[
            pltpu.VMEM((n_head, 2, share, depth), bf16),
            dma((2, n_head)),
            dma((2, n_rail, n_head)),
            dma((2, n_rail, n_head)),
            dma((2, n_rail, n_head)),
        ],
        compiler_params=pltpu.CompilerParams(
            collective_id=0, has_side_effects=True, vmem_limit_bytes=VMEM_LIMIT
        ),
        name="gather_rows",
    )(key_proj.reshape(share, kv_heads * depth), value_proj.reshape(share, kv_heads * depth))

    rows = TILE * group
    per_shard = row_count // TILE
    most = tiles // 4
    smem = pl.BlockSpec(memory_space=pltpu.SMEM)
    tile_spec = pl.BlockSpec((rows, depth), lambda t: (t, 0))
    attended, query_grad, partial = pl.pallas_call(
        functools.partial(attention_kernel, tiles, group, docs),
        grid=(per_shard,),
        out_shape=(
            jax.ShapeDtypeStruct((row_count * group, depth), bf16),
            jax.ShapeDtypeStruct((row_count * group, depth), bf16),
            jax.ShapeDtypeStruct((2, tiles, TILE, depth), bf16),
        ),
        in_specs=[smem, smem, tile_spec, tile_spec, vmem],
        out_specs=(tile_spec, tile_spec, vmem),
        scratch_shapes=[
            pltpu.SMEM((tiles,), jnp.int32),
            pltpu.VMEM((tiles, depth, TILE), bf16),
            pltpu.VMEM((tiles, depth, TILE), bf16),
            pltpu.VMEM((depth, rows), bf16),
            pltpu.VMEM((depth, rows), bf16),
            pltpu.VMEM((rows, depth), bf16),
            pltpu.VMEM((depth, rows), bf16),
            pltpu.VMEM((most, 2 * TILE, rows), f32),
            pltpu.VMEM((most, 2 * TILE, rows), bf16),
            pltpu.VMEM((depth, rows), f32),
            pltpu.VMEM((depth, rows), f32),
            pltpu.VMEM((2, tiles, TILE, depth), f32),
            pltpu.VMEM((TILE, rows), jnp.int32),
        ],
        compiler_params=pltpu.CompilerParams(vmem_limit_bytes=VMEM_LIMIT),
        name="attention_tiles",
    )(
        tile_order,
        doc_tiles,
        queries.reshape(row_count * group, depth),
        out_grad.reshape(row_count * group, depth),
        rows_kv.reshape(2, tiles, TILE, depth),
    )

    key_grad, value_grad = pl.pallas_call(
        functools.partial(reduce_kernel, n_ctx, n_head),
        out_shape=(
            jax.ShapeDtypeStruct((share, kv_heads * depth), bf16),
            jax.ShapeDtypeStruct((share, kv_heads * depth), bf16),
        ),
        in_specs=[vmem],
        out_specs=(vmem, vmem),
        scratch_shapes=[
            pltpu.VMEM((n_rail, 2, n_head, share, depth), bf16),
            pltpu.VMEM((n_rail, n_head, 2, share, depth), bf16),
            pltpu.VMEM((n_rail, n_head, 2, share, depth), bf16),
            pltpu.VMEM((n_rail, n_head, 2, share, depth), bf16),
            pltpu.VMEM((n_rail, n_head, 2, share, depth), bf16),
            pltpu.VMEM((n_head, 2, share, depth), bf16),
            pltpu.VMEM((n_head, 2, share, depth), bf16),
            dma((2, n_rail)),
            dma((2, n_rail, n_head)),
            dma((2, n_rail, n_head)),
            dma((2, n_head)),
        ],
        compiler_params=pltpu.CompilerParams(
            collective_id=1, has_side_effects=True, vmem_limit_bytes=VMEM_LIMIT
        ),
        name="sum_gradients",
    )(partial.reshape(2, n_ctx, n_head, share, depth))

    return (
        attended.reshape(row_count, group, depth),
        query_grad.reshape(row_count, group, depth),
        key_grad.reshape(share, kv_heads, depth),
        value_grad.reshape(share, kv_heads, depth),
    )


def solution(mesh):
    in_specs = (
        P("ctx", "head", None),
        P(("ctx", "head"), None, None),
        P(("ctx", "head"), None, None),
        P("ctx", "head", None),
        P(),
        P(),
    )
    out_specs = (
        P("ctx", "head", None),
        P("ctx", "head", None),
        P(("ctx", "head"), None, None),
        P(("ctx", "head"), None, None),
    )
    return jax.shard_map(
        functools.partial(body, mesh.shape["ctx"], mesh.shape["head"]),
        mesh=mesh,
        in_specs=in_specs,
        out_specs=out_specs,
        check_vma=False,
    )
```

```python
import functools
import math

import jax
import jax.numpy as jnp
from jax import lax
from jax.experimental import pallas as pl
from jax.experimental.pallas import tpu as pltpu
from jax.sharding import PartitionSpec as P

TILE = 128
NEG = -1e30
MESH = pl.DeviceIdType.MESH
VMEM_LIMIT = 48 * 1024 * 1024


def peers(n_ctx, n_head):
    ctx = lax.axis_index("ctx")
    head = lax.axis_index("head")
    core = lax.rem(ctx, 2)
    rail = lax.div(ctx, 2)
    n_rail = n_ctx // 2
    sibling = rail * 2 + (1 - core)
    return ctx, head, core, rail, n_rail, sibling


def entry_barrier(ctx, head, core, rail, n_rail, sibling, n_head):
    barrier = pltpu.get_barrier_semaphore()
    for d in range(1, n_head):
        pl.semaphore_signal(
            barrier, inc=1, device_id=(ctx, lax.rem(head + d, n_head)), device_id_type=MESH
        )
    for d in range(1, n_rail):
        pl.semaphore_signal(
            barrier,
            inc=1,
            device_id=(lax.rem(rail + d, n_rail) * 2 + core, head),
            device_id_type=MESH,
        )
    pl.semaphore_signal(barrier, inc=1, device_id=(sibling, head), device_id_type=MESH)
    pl.semaphore_wait(barrier, n_head - 1 + n_rail - 1 + 1)


def remote(src, dst, send, recv, ctx, head):
    return pltpu.make_async_remote_copy(
        src_ref=src,
        dst_ref=dst,
        send_sem=send,
        recv_sem=recv,
        device_id=(ctx, head),
        device_id_type=MESH,
    )


def dot(a, b):
    return jnp.dot(a, b, preferred_element_type=jnp.float32)


def fused_kernel(
    n_ctx, n_head, tiles, group, docs, per_shard, share,
    order_ref, docs_ref, q_ref, g_ref, k_ref, v_ref,
    o_ref, dq_ref, kg_ref, vg_ref,
    slots, turned, k_buf, v_buf, kw, kw_t, vw, vw_t, q_t, g_t, g_s, weights, dscores, o_t,
    inverse, delta, dkw, dvw, part_k, part_v, sib_k, sib_v, out_k, out_v, in_k, in_v,
    back, head_in,
    head_sems, rail_sems, sib_sems, fwd_sems, psib_sems, prail_sems, phead_sems,
):
    f32, bf16 = jnp.float32, jnp.bfloat16
    ctx, head, core, rail, n_rail, sibling = peers(n_ctx, n_head)
    parts = TILE // share
    window = tiles // 2
    total_chunks, chunk, depth = q_ref.shape
    chunks = total_chunks // per_shard
    scale = 1.0 / math.sqrt(depth)
    bufs = (k_buf, v_buf)

    def rows_of(buf, c, h):
        return buf.at[c * per_shard + lax.div(h, parts), lax.rem(h, parts)]

    def rail_at(dz):
        return lax.rem(rail + dz, n_rail) * 2 + core

    for x, source in enumerate((k_ref, v_ref)):
        for g in range(n_head):
            turned[x, g] = source[:, g * depth : (g + 1) * depth]
    for x in range(2):
        bufs[x][ctx * per_shard + lax.div(head, parts), lax.rem(head, parts)] = turned[x, head]
    entry_barrier(ctx, head, core, rail, n_rail, sibling, n_head)

    def head_copy(x, d):
        target = lax.rem(head + d, n_head)
        return remote(
            turned.at[x, target], rows_of(bufs[x], ctx, head), head_sems.at[x, 0, d],
            head_sems.at[x, 1, d], ctx, target,
        )

    def rail_copy(x, dz, d):
        rows = rows_of(bufs[x], ctx, lax.rem(head + n_head - d, n_head))
        return remote(
            rows, rows, rail_sems.at[x, 0, dz, d], rail_sems.at[x, 1, dz, d], rail_at(dz), head
        )

    def sib_copy(x, d):
        rows = rows_of(bufs[x], ctx, lax.rem(head + n_head - d, n_head))
        return remote(rows, rows, sib_sems.at[x, 0, d], sib_sems.at[x, 1, d], sibling, head)

    def fwd_copy(x, dz):
        source = lax.rem(rail + n_rail - dz, n_rail) * 2 + core
        rows = bufs[x].at[pl.ds(source * per_shard, per_shard)]
        return remote(rows, rows, fwd_sems.at[x, 0, dz], fwd_sems.at[x, 1, dz], sibling, head)

    def hand_on(x):
        for dz in range(1, n_rail):
            for d in range(n_head):
                rail_copy(x, dz, d).wait_recv()
            fwd_copy(x, dz).start()

    def arrive(x):
        for d in range(n_head):
            sib_copy(x, d).wait_recv()
        for dz in range(1, n_rail):
            fwd_copy(x, dz).wait_recv()

    for x in range(2):
        for d in range(1, n_head):
            head_copy(x, d).start()
    for x in range(2):
        for d in range(n_head):
            if d > 0:
                head_copy(x, d).wait_recv()
            for dz in range(n_rail - 1, 0, -1):
                rail_copy(x, dz, d).start()
            sib_copy(x, d).start()

    mine, count = [], []
    for t in range(per_shard):
        tile = order_ref[ctx * per_shard + t]
        end, first = 0, 0
        for d in range(docs):
            end = end + docs_ref[d]
            first = jnp.where(end <= tile, end, first)
        mine.append(tile)
        count.append(tile - first + 1)
        for w in range(window):
            wanted = jnp.maximum(tile - w, 0)
            slot = 0
            for s in range(tiles):
                slot = jnp.where(order_ref[s] == wanted, s, slot)
            slots[t * window + w] = slot
        dkw[t, window] = jnp.zeros((TILE, depth), f32)
        dvw[t, window] = jnp.zeros((TILE, depth), f32)

    @pl.loop(0, total_chunks)
    def _(n):
        q_t[n] = q_ref[n].T
        g_t[n] = g_ref[n].T

    def fill(into, turned_into, buf):
        for t in range(per_shard):
            @pl.loop(0, window)
            def _(w):
                block = buf[slots[t * window + w]].reshape(TILE, depth)
                into[t, w] = block
                turned_into[t, w] = block.T

    hand_on(0)
    arrive(0)
    fill(kw, kw_t, k_buf)

    for t in range(per_shard):
        @pl.loop(t * chunks, (t + 1) * chunks)
        def _(n):
            s = dot(kw[t].reshape(window * TILE, depth), q_t[n])
            key = lax.broadcasted_iota(jnp.int32, (TILE, chunk), 0)
            row = lax.div(lax.broadcasted_iota(jnp.int32, (TILE, chunk), 1), group)
            seen = key - row <= (n - t * chunks) * (chunk // group)
            pieces = [jnp.where(seen, s[:TILE], NEG)]
            for w in range(1, window):
                pieces.append(s[w * TILE : (w + 1) * TILE] + jnp.where(w < count[t], 0.0, NEG))
            top = pieces[0]
            for piece in pieces[1:]:
                top = jnp.maximum(top, piece)
            top = jnp.max(top, axis=0, keepdims=True)
            total = jnp.zeros((TILE, chunk), f32)
            for w, piece in enumerate(pieces):
                e = jnp.exp2((piece - top) * (scale * math.log2(math.e)))
                total = total + e
                weights[n, w * TILE : (w + 1) * TILE] = e.astype(bf16)
            inverse[n] = 1.0 / jnp.sum(total, axis=0, keepdims=True)

    hand_on(1)
    arrive(1)
    fill(vw, vw_t, v_buf)

    def side(ref, t):
        return jnp.concatenate([ref[t, w] for w in range(window)], axis=1)

    for t in range(per_shard):
        @pl.loop(t * chunks, (t + 1) * chunks)
        def _(n):
            out = (dot(side(vw_t, t), weights[n]) * inverse[n]).astype(bf16)
            o_t[n] = out
            grads = g_t[n].astype(f32)
            delta[n] = jnp.sum(grads * out.astype(f32), axis=0, keepdims=True) * inverse[n]
            scaled = (grads * inverse[n]).astype(bf16)
            g_t[n] = scaled
            g_s[n] = scaled.T

    def by_key(into, left, right):
        for t in range(per_shard):
            total = dot(left[t * chunks], right[t * chunks])
            for c in range(1, chunks):
                total = total + dot(left[t * chunks + c], right[t * chunks + c])
            into[t, 0:window] = total.reshape(window, TILE, depth)

    def by_slot(part, by_window):
        @pl.loop(0, tiles)
        def _(s):
            total = None
            for t in range(per_shard):
                w = mine[t] - order_ref[s]
                term = by_window[t, jnp.where((w >= 0) & (w < count[t]), w, window)]
                total = term if total is None else total + term
            part[s] = total.astype(bf16).reshape(parts, share, depth)

    part = (part_k, part_v)
    sib_in = (sib_k, sib_v)
    outs = (out_k, out_v)
    ins = (in_k, in_v)

    def psib_copy(x, dz):
        rows = part[x].at[pl.ds((lax.rem(rail + dz, n_rail) * 2 + 1 - core) * per_shard, per_shard)]
        return remote(
            rows, sib_in[x].at[dz], psib_sems.at[x, 0, dz], psib_sems.at[x, 1, dz], sibling, head
        )

    def prail_copy(x, dz):
        return remote(
            outs[x].at[dz], ins[x].at[dz], prail_sems.at[x, 0, dz], prail_sems.at[x, 1, dz],
            rail_at(dz), head,
        )

    def phead_copy(x, d):
        target = lax.rem(head + d, n_head)
        return remote(
            back.at[x, target], head_in.at[x, d], phead_sems.at[x, 0, d], phead_sems.at[x, 1, d],
            ctx, target,
        )

    far_first = list(range(n_rail - 1, -1, -1))

    def to_sibling(x):
        for dz in far_first:
            psib_copy(x, dz).start()

    def pair_sum(x, dz):
        own = part[x][pl.ds(rail_at(dz) * per_shard, per_shard)].astype(f32)
        return own + sib_in[x][dz].astype(f32)

    def to_rail(x):
        for dz in far_first[:-1]:
            psib_copy(x, dz).wait_recv()
            outs[x][dz] = pair_sum(x, dz).astype(bf16)
            prail_copy(x, dz).start()

    def to_heads(x, factor):
        psib_copy(x, 0).wait_recv()
        total = pair_sum(x, 0)
        for dz in range(1, n_rail):
            prail_copy(x, dz).wait_recv()
            total = total + ins[x][dz].astype(f32)
        if factor is not None:
            total = total * factor
        total = total.astype(bf16)
        for g in range(n_head):
            back[x, g] = total[g // parts, g % parts]
        for d in range(1, n_head):
            phead_copy(x, d).start()
        head_in[x, 0] = back[x, head]

    by_key(dvw, weights, g_s)
    by_slot(part_v, dvw)
    to_sibling(1)
    for t in range(per_shard):
        @pl.loop(t * chunks, (t + 1) * chunks)
        def _(n):
            dp = dot(vw[t].reshape(window * TILE, depth), g_t[n])
            dscores[n] = (weights[n].astype(f32) * (dp - delta[n])).astype(bf16)
    to_rail(1)
    by_key(dkw, dscores, q_ref)
    by_slot(part_k, dkw)
    to_sibling(0)

    @pl.loop(0, total_chunks)
    def _(n):
        o_ref[n] = o_t[n].T
    to_rail(0)
    for t in range(per_shard):
        @pl.loop(t * chunks, (t + 1) * chunks)
        def _(n):
            dq_ref[n] = (dot(side(kw_t, t), dscores[n]) * scale).astype(bf16).T
    to_heads(1, None)
    to_heads(0, scale)
    for x, result in ((1, vg_ref), (0, kg_ref)):
        for d in range(1, n_head):
            phead_copy(x, d).wait_recv()
        for g in range(n_head):
            place = lax.rem(head - g + n_head, n_head)
            result[:, g * depth : (g + 1) * depth] = head_in[x, place]

    for x in range(2):
        for d in range(n_head):
            if d > 0:
                head_copy(x, d).wait_send()
                phead_copy(x, d).wait_send()
            for dz in range(1, n_rail):
                rail_copy(x, dz, d).wait_send()
            sib_copy(x, d).wait_send()
        for dz in range(n_rail):
            psib_copy(x, dz).wait_send()
            if dz > 0:
                fwd_copy(x, dz).wait_send()
                prail_copy(x, dz).wait_send()


def body(n_ctx, n_head, queries, key_proj, value_proj, out_grad, tile_order, doc_tiles):
    row_count, group, depth = queries.shape
    share, kv_heads, _ = key_proj.shape
    tiles = tile_order.shape[0]
    docs = doc_tiles.shape[0]
    n_rail = n_ctx // 2
    per_shard = row_count // TILE
    parts = TILE // share
    window = tiles // 2
    chunk = 256
    nch = row_count * group // chunk
    bf16, f32 = jnp.bfloat16, jnp.float32
    vmem = pl.BlockSpec(memory_space=pltpu.VMEM)
    smem = pl.BlockSpec(memory_space=pltpu.SMEM)
    dma = pltpu.SemaphoreType.DMA
    wide = jax.ShapeDtypeStruct((nch, chunk, depth), bf16)
    thin = jax.ShapeDtypeStruct((share, kv_heads * depth), bf16)
    shard = (per_shard, parts, share, depth)
    attended, query_grad, key_grad, value_grad = pl.pallas_call(
        functools.partial(fused_kernel, n_ctx, n_head, tiles, group, docs, per_shard, share),
        out_shape=(wide, wide, thin, thin),
        in_specs=[smem, smem, vmem, vmem, vmem, vmem],
        out_specs=(vmem, vmem, vmem, vmem),
        scratch_shapes=[
            pltpu.SMEM((per_shard * window,), jnp.int32),
            pltpu.VMEM((2, n_head, share, depth), bf16),
            pltpu.VMEM((tiles, parts, share, depth), bf16),
            pltpu.VMEM((tiles, parts, share, depth), bf16),
            pltpu.VMEM((per_shard, window, TILE, depth), bf16),
            pltpu.VMEM((per_shard, window, depth, TILE), bf16),
            pltpu.VMEM((per_shard, window, TILE, depth), bf16),
            pltpu.VMEM((per_shard, window, depth, TILE), bf16),
            pltpu.VMEM((nch, depth, chunk), bf16),
            pltpu.VMEM((nch, depth, chunk), bf16),
            pltpu.VMEM((nch, chunk, depth), bf16),
            pltpu.VMEM((nch, window * TILE, chunk), bf16),
            pltpu.VMEM((nch, window * TILE, chunk), bf16),
            pltpu.VMEM((nch, depth, chunk), bf16),
            pltpu.VMEM((nch, 1, chunk), f32),
            pltpu.VMEM((nch, 1, chunk), f32),
            pltpu.VMEM((per_shard, window + 1, TILE, depth), f32),
            pltpu.VMEM((per_shard, window + 1, TILE, depth), f32),
            pltpu.VMEM((tiles, parts, share, depth), bf16),
            pltpu.VMEM((tiles, parts, share, depth), bf16),
        ]
        + [pltpu.VMEM((n_rail,) + shard, bf16)] * 6
        + [
            pltpu.VMEM((2, n_head, share, depth), bf16),
            pltpu.VMEM((2, n_head, share, depth), bf16),
            dma((2, 2, n_head)),
            dma((2, 2, n_rail, n_head)),
            dma((2, 2, n_head)),
            dma((2, 2, n_rail)),
            dma((2, 2, n_rail)),
            dma((2, 2, n_rail)),
            dma((2, 2, n_head)),
        ],
        compiler_params=pltpu.CompilerParams(
            collective_id=0, has_side_effects=True, vmem_limit_bytes=VMEM_LIMIT
        ),
        name="attention_all",
    )(
        tile_order,
        doc_tiles,
        queries.reshape(nch, chunk, depth),
        out_grad.reshape(nch, chunk, depth),
        key_proj.reshape(share, kv_heads * depth),
        value_proj.reshape(share, kv_heads * depth),
    )
    return (
        attended.reshape(row_count, group, depth),
        query_grad.reshape(row_count, group, depth),
        key_grad.reshape(share, kv_heads, depth),
        value_grad.reshape(share, kv_heads, depth),
    )


def solution(mesh):
    in_specs = (
        P("ctx", "head", None),
        P(("ctx", "head"), None, None),
        P(("ctx", "head"), None, None),
        P("ctx", "head", None),
        P(),
        P(),
    )
    out_specs = (
        P("ctx", "head", None),
        P("ctx", "head", None),
        P(("ctx", "head"), None, None),
        P(("ctx", "head"), None, None),
    )
    return jax.shard_map(
        functools.partial(body, mesh.shape["ctx"], mesh.shape["head"]),
        mesh=mesh,
        in_specs=in_specs,
        out_specs=out_specs,
        check_vma=False,
    )
```

```python
import functools
import math

import jax
import jax.numpy as jnp
from jax import lax
from jax.experimental import pallas as pl
from jax.experimental.pallas import tpu as pltpu
from jax.sharding import PartitionSpec as P

TILE = 128
NEG = -1e30
MESH = pl.DeviceIdType.MESH
VMEM_LIMIT = 48 * 1024 * 1024


def peers(n_ctx, n_head):
    ctx = lax.axis_index("ctx")
    head = lax.axis_index("head")
    core = lax.rem(ctx, 2)
    rail = lax.div(ctx, 2)
    n_rail = n_ctx // 2
    sibling = rail * 2 + (1 - core)
    return ctx, head, core, rail, n_rail, sibling


def entry_barrier(ctx, head, core, rail, n_rail, sibling, n_head):
    barrier = pltpu.get_barrier_semaphore()
    for d in range(1, n_head):
        pl.semaphore_signal(
            barrier, inc=1, device_id=(ctx, lax.rem(head + d, n_head)), device_id_type=MESH
        )
    for d in range(1, n_rail):
        pl.semaphore_signal(
            barrier,
            inc=1,
            device_id=(lax.rem(rail + d, n_rail) * 2 + core, head),
            device_id_type=MESH,
        )
    pl.semaphore_signal(barrier, inc=1, device_id=(sibling, head), device_id_type=MESH)
    pl.semaphore_wait(barrier, n_head - 1 + n_rail - 1 + 1)


def remote(src, dst, send, recv, ctx, head):
    return pltpu.make_async_remote_copy(
        src_ref=src,
        dst_ref=dst,
        send_sem=send,
        recv_sem=recv,
        device_id=(ctx, head),
        device_id_type=MESH,
    )


def dot(a, b):
    return jnp.dot(a, b, preferred_element_type=jnp.float32)


def fused_kernel(
    n_ctx, n_head, tiles, group, docs, per_shard, share,
    order_ref, docs_ref, q_ref, g_ref, k_ref, v_ref,
    o_ref, dq_ref, kg_ref, vg_ref,
    slots, turned, k_buf, v_buf, kw, kw_t, vw, vw_t, q_t, g_t, g_s, weights, dscores, o_t,
    inverse, delta, dkw, dvw, part_k, part_v, sib_k, sib_v, out_k, out_v, in_k, in_v,
    back, head_in,
    head_sems, rail_sems, sib_sems, fwd_sems, psib_sems, prail_sems, phead_sems,
):
    f32, bf16 = jnp.float32, jnp.bfloat16
    ctx, head, core, rail, n_rail, sibling = peers(n_ctx, n_head)
    parts = TILE // share
    window = tiles // 2
    total_chunks, chunk, depth = q_ref.shape
    chunks = total_chunks // per_shard
    scale = 1.0 / math.sqrt(depth)
    bufs = (k_buf, v_buf)

    def rows_of(buf, c, h):
        return buf.at[c * per_shard + lax.div(h, parts), lax.rem(h, parts)]

    def rail_at(dz):
        return lax.rem(rail + dz, n_rail) * 2 + core

    for x, source in enumerate((k_ref, v_ref)):
        for g in range(n_head):
            turned[x, g] = source[:, g * depth : (g + 1) * depth]
    for x in range(2):
        bufs[x][ctx * per_shard + lax.div(head, parts), lax.rem(head, parts)] = turned[x, head]
    entry_barrier(ctx, head, core, rail, n_rail, sibling, n_head)

    def head_copy(x, d):
        target = lax.rem(head + d, n_head)
        return remote(
            turned.at[x, target], rows_of(bufs[x], ctx, head), head_sems.at[x, 0, d],
            head_sems.at[x, 1, d], ctx, target,
        )

    def rail_copy(x, dz, d):
        rows = rows_of(bufs[x], ctx, lax.rem(head + n_head - d, n_head))
        return remote(
            rows, rows, rail_sems.at[x, 0, dz, d], rail_sems.at[x, 1, dz, d], rail_at(dz), head
        )

    def sib_copy(x, d):
        rows = rows_of(bufs[x], ctx, lax.rem(head + n_head - d, n_head))
        return remote(rows, rows, sib_sems.at[x, 0, d], sib_sems.at[x, 1, d], sibling, head)

    def fwd_copy(x, dz):
        source = lax.rem(rail + n_rail - dz, n_rail) * 2 + core
        rows = bufs[x].at[pl.ds(source * per_shard, per_shard)]
        return remote(rows, rows, fwd_sems.at[x, 0, dz], fwd_sems.at[x, 1, dz], sibling, head)

    def hand_on(x):
        for dz in range(1, n_rail):
            for d in range(n_head):
                rail_copy(x, dz, d).wait_recv()
            fwd_copy(x, dz).start()

    def arrive(x):
        for d in range(n_head):
            sib_copy(x, d).wait_recv()
        for dz in range(1, n_rail):
            fwd_copy(x, dz).wait_recv()

    for x in range(2):
        for d in range(1, n_head):
            head_copy(x, d).start()
    def spread(x):
        for d in range(n_head):
            if d > 0:
                head_copy(x, d).wait_recv()
            for dz in range(n_rail - 1, 0, -1):
                rail_copy(x, dz, d).start()
            sib_copy(x, d).start()

    spread(0)

    mine, count = [], []
    for t in range(per_shard):
        tile = order_ref[ctx * per_shard + t]
        end, first = 0, 0
        for d in range(docs):
            end = end + docs_ref[d]
            first = jnp.where(end <= tile, end, first)
        mine.append(tile)
        count.append(tile - first + 1)
        for w in range(window):
            wanted = jnp.maximum(tile - w, 0)
            slot = 0
            for s in range(tiles):
                slot = jnp.where(order_ref[s] == wanted, s, slot)
            slots[t * window + w] = slot
        dkw[t, window] = jnp.zeros((TILE, depth), f32)
        dvw[t, window] = jnp.zeros((TILE, depth), f32)

    @pl.loop(0, total_chunks)
    def _(n):
        q_t[n] = q_ref[n].T
        g_t[n] = g_ref[n].T

    def fill(into, turned_into, buf):
        for t in range(per_shard):
            @pl.loop(0, window)
            def _(w):
                block = buf[slots[t * window + w]].reshape(TILE, depth)
                into[t, w] = block
                turned_into[t, w] = block.T

    hand_on(0)
    spread(1)
    arrive(0)
    fill(kw, kw_t, k_buf)

    for t in range(per_shard):
        @pl.loop(t * chunks, (t + 1) * chunks)
        def _(n):
            s = dot(kw[t].reshape(window * TILE, depth), q_t[n])
            key = lax.broadcasted_iota(jnp.int32, (TILE, chunk), 0)
            row = lax.div(lax.broadcasted_iota(jnp.int32, (TILE, chunk), 1), group)
            seen = key - row <= (n - t * chunks) * (chunk // group)
            pieces = [jnp.where(seen, s[:TILE], NEG)]
            for w in range(1, window):
                pieces.append(s[w * TILE : (w + 1) * TILE] + jnp.where(w < count[t], 0.0, NEG))
            top = pieces[0]
            for piece in pieces[1:]:
                top = jnp.maximum(top, piece)
            top = jnp.max(top, axis=0, keepdims=True)
            total = jnp.zeros((TILE, chunk), f32)
            for w, piece in enumerate(pieces):
                e = jnp.exp2((piece - top) * (scale * math.log2(math.e)))
                total = total + e
                weights[n, w * TILE : (w + 1) * TILE] = e.astype(bf16)
            inverse[n] = 1.0 / jnp.sum(total, axis=0, keepdims=True)

    hand_on(1)
    arrive(1)
    fill(vw, vw_t, v_buf)

    def side(ref, t):
        return jnp.concatenate([ref[t, w] for w in range(window)], axis=1)

    for t in range(per_shard):
        @pl.loop(t * chunks, (t + 1) * chunks)
        def _(n):
            out = (dot(side(vw_t, t), weights[n]) * inverse[n]).astype(bf16)
            o_t[n] = out
            grads = g_t[n].astype(f32)
            delta[n] = jnp.sum(grads * out.astype(f32), axis=0, keepdims=True) * inverse[n]
            scaled = (grads * inverse[n]).astype(bf16)
            g_t[n] = scaled
            g_s[n] = scaled.T

    def by_key(into, left, right):
        for t in range(per_shard):
            total = dot(left[t * chunks], right[t * chunks])
            for c in range(1, chunks):
                total = total + dot(left[t * chunks + c], right[t * chunks + c])
            into[t, 0:window] = total.reshape(window, TILE, depth)

    def by_slot(part, by_window):
        @pl.loop(0, tiles)
        def _(s):
            total = None
            for t in range(per_shard):
                w = mine[t] - order_ref[s]
                term = by_window[t, jnp.where((w >= 0) & (w < count[t]), w, window)]
                total = term if total is None else total + term
            part[s] = total.astype(bf16).reshape(parts, share, depth)

    part = (part_k, part_v)
    sib_in = (sib_k, sib_v)
    outs = (out_k, out_v)
    ins = (in_k, in_v)

    def psib_copy(x, dz):
        rows = part[x].at[pl.ds((lax.rem(rail + dz, n_rail) * 2 + 1 - core) * per_shard, per_shard)]
        return remote(
            rows, sib_in[x].at[dz], psib_sems.at[x, 0, dz], psib_sems.at[x, 1, dz], sibling, head
        )

    def prail_copy(x, dz):
        return remote(
            outs[x].at[dz], ins[x].at[dz], prail_sems.at[x, 0, dz], prail_sems.at[x, 1, dz],
            rail_at(dz), head,
        )

    def phead_copy(x, d):
        target = lax.rem(head + d, n_head)
        return remote(
            back.at[x, target], head_in.at[x, d], phead_sems.at[x, 0, d], phead_sems.at[x, 1, d],
            ctx, target,
        )

    far_first = list(range(n_rail - 1, -1, -1))

    def to_sibling(x):
        for dz in far_first:
            psib_copy(x, dz).start()

    def pair_sum(x, dz):
        own = part[x][pl.ds(rail_at(dz) * per_shard, per_shard)].astype(f32)
        return own + sib_in[x][dz].astype(f32)

    def to_rail(x):
        for dz in far_first[:-1]:
            psib_copy(x, dz).wait_recv()
            outs[x][dz] = pair_sum(x, dz).astype(bf16)
            prail_copy(x, dz).start()

    def to_heads(x, factor):
        psib_copy(x, 0).wait_recv()
        total = pair_sum(x, 0)
        for dz in range(1, n_rail):
            prail_copy(x, dz).wait_recv()
            total = total + ins[x][dz].astype(f32)
        if factor is not None:
            total = total * factor
        total = total.astype(bf16)
        for g in range(n_head):
            back[x, g] = total[g // parts, g % parts]
        for d in range(1, n_head):
            phead_copy(x, d).start()
        head_in[x, 0] = back[x, head]

    by_key(dvw, weights, g_s)
    by_slot(part_v, dvw)
    to_sibling(1)
    for t in range(per_shard):
        @pl.loop(t * chunks, (t + 1) * chunks)
        def _(n):
            dp = dot(vw[t].reshape(window * TILE, depth), g_t[n])
            dscores[n] = (weights[n].astype(f32) * (dp - delta[n])).astype(bf16)
    to_rail(1)
    by_key(dkw, dscores, q_ref)
    by_slot(part_k, dkw)
    to_sibling(0)

    @pl.loop(0, total_chunks)
    def _(n):
        o_ref[n] = o_t[n].T
    to_rail(0)
    for t in range(per_shard):
        @pl.loop(t * chunks, (t + 1) * chunks)
        def _(n):
            dq_ref[n] = (dot(side(kw_t, t), dscores[n]) * scale).astype(bf16).T
    to_heads(1, None)
    to_heads(0, scale)
    for x, result in ((1, vg_ref), (0, kg_ref)):
        for d in range(1, n_head):
            phead_copy(x, d).wait_recv()
        for g in range(n_head):
            place = lax.rem(head - g + n_head, n_head)
            result[:, g * depth : (g + 1) * depth] = head_in[x, place]

    for x in range(2):
        for d in range(n_head):
            if d > 0:
                head_copy(x, d).wait_send()
                phead_copy(x, d).wait_send()
            for dz in range(1, n_rail):
                rail_copy(x, dz, d).wait_send()
            sib_copy(x, d).wait_send()
        for dz in range(n_rail):
            psib_copy(x, dz).wait_send()
            if dz > 0:
                fwd_copy(x, dz).wait_send()
                prail_copy(x, dz).wait_send()


def body(n_ctx, n_head, queries, key_proj, value_proj, out_grad, tile_order, doc_tiles):
    row_count, group, depth = queries.shape
    share, kv_heads, _ = key_proj.shape
    tiles = tile_order.shape[0]
    docs = doc_tiles.shape[0]
    n_rail = n_ctx // 2
    per_shard = row_count // TILE
    parts = TILE // share
    window = tiles // 2
    chunk = 256
    nch = row_count * group // chunk
    bf16, f32 = jnp.bfloat16, jnp.float32
    vmem = pl.BlockSpec(memory_space=pltpu.VMEM)
    smem = pl.BlockSpec(memory_space=pltpu.SMEM)
    dma = pltpu.SemaphoreType.DMA
    wide = jax.ShapeDtypeStruct((nch, chunk, depth), bf16)
    thin = jax.ShapeDtypeStruct((share, kv_heads * depth), bf16)
    shard = (per_shard, parts, share, depth)
    attended, query_grad, key_grad, value_grad = pl.pallas_call(
        functools.partial(fused_kernel, n_ctx, n_head, tiles, group, docs, per_shard, share),
        out_shape=(wide, wide, thin, thin),
        in_specs=[smem, smem, vmem, vmem, vmem, vmem],
        out_specs=(vmem, vmem, vmem, vmem),
        scratch_shapes=[
            pltpu.SMEM((per_shard * window,), jnp.int32),
            pltpu.VMEM((2, n_head, share, depth), bf16),
            pltpu.VMEM((tiles, parts, share, depth), bf16),
            pltpu.VMEM((tiles, parts, share, depth), bf16),
            pltpu.VMEM((per_shard, window, TILE, depth), bf16),
            pltpu.VMEM((per_shard, window, depth, TILE), bf16),
            pltpu.VMEM((per_shard, window, TILE, depth), bf16),
            pltpu.VMEM((per_shard, window, depth, TILE), bf16),
            pltpu.VMEM((nch, depth, chunk), bf16),
            pltpu.VMEM((nch, depth, chunk), bf16),
            pltpu.VMEM((nch, chunk, depth), bf16),
            pltpu.VMEM((nch, window * TILE, chunk), bf16),
            pltpu.VMEM((nch, window * TILE, chunk), bf16),
            pltpu.VMEM((nch, depth, chunk), bf16),
            pltpu.VMEM((nch, 1, chunk), f32),
            pltpu.VMEM((nch, 1, chunk), f32),
            pltpu.VMEM((per_shard, window + 1, TILE, depth), f32),
            pltpu.VMEM((per_shard, window + 1, TILE, depth), f32),
            pltpu.VMEM((tiles, parts, share, depth), bf16),
            pltpu.VMEM((tiles, parts, share, depth), bf16),
        ]
        + [pltpu.VMEM((n_rail,) + shard, bf16)] * 6
        + [
            pltpu.VMEM((2, n_head, share, depth), bf16),
            pltpu.VMEM((2, n_head, share, depth), bf16),
            dma((2, 2, n_head)),
            dma((2, 2, n_rail, n_head)),
            dma((2, 2, n_head)),
            dma((2, 2, n_rail)),
            dma((2, 2, n_rail)),
            dma((2, 2, n_rail)),
            dma((2, 2, n_head)),
        ],
        compiler_params=pltpu.CompilerParams(
            collective_id=0, has_side_effects=True, vmem_limit_bytes=VMEM_LIMIT
        ),
        name="attention_all",
    )(
        tile_order,
        doc_tiles,
        queries.reshape(nch, chunk, depth),
        out_grad.reshape(nch, chunk, depth),
        key_proj.reshape(share, kv_heads * depth),
        value_proj.reshape(share, kv_heads * depth),
    )
    return (
        attended.reshape(row_count, group, depth),
        query_grad.reshape(row_count, group, depth),
        key_grad.reshape(share, kv_heads, depth),
        value_grad.reshape(share, kv_heads, depth),
    )


def solution(mesh):
    in_specs = (
        P("ctx", "head", None),
        P(("ctx", "head"), None, None),
        P(("ctx", "head"), None, None),
        P("ctx", "head", None),
        P(),
        P(),
    )
    out_specs = (
        P("ctx", "head", None),
        P("ctx", "head", None),
        P(("ctx", "head"), None, None),
        P(("ctx", "head"), None, None),
    )
    return jax.shard_map(
        functools.partial(body, mesh.shape["ctx"], mesh.shape["head"]),
        mesh=mesh,
        in_specs=in_specs,
        out_specs=out_specs,
        check_vma=False,
    )
```
